32 devices in a mesh: groups: 1, px: 32 (over z, y, x, core).
Axes of the slice: x: 2, y: 2, z: 4, core: 2. Of those that a mesh axis runs over, the one named last changes fastest.
Arguments:
- features: bfloat16 [1, 10, 256, 256, 256], P('groups', None, 'px'), may hold values from -6 to 6
- cotangent: bfloat16 [1, 10, 256, 256, 256], P('groups', None, 'px'), may hold values from -6 to 6
- spectral_weight: bfloat16 [2, 10, 10, 221184], P(None, None, None, 'px'), may hold values from -1.25 to 1.25
- pointwise_weight: bfloat16 [10, 10], replicated, may hold values from -2 to 2
- bias_term: float32 [10], replicated, may hold values from -3 to 3
Outputs:
- layer_out: bfloat16 [1, 10, 256, 256, 256], P('groups', None, 'px')
- feature_grad: bfloat16 [1, 10, 256, 256, 256], P('groups', None, 'px')
- weight_grad: float32 [2, 10, 10, 221184], P('groups', None, None, 'px')
The draws below stay inside these ranges and needn't reach their ends.
All inputs are finite; a program needn't handle non-finite values.
Results may differ from the reference program's by a relative error of at most 0.0072.
The reference program's roundings to bfloat16 on the way (of `zt_basis`) count: a program that leaves them out, or rounds other values in their place, can miss the bound.
Values may be sent and summed in bfloat16 or wider, within the bound.
A program may use at most 384 MiB of HBM per device.

```python
import math
import jax
import jax.numpy as jnp
from jax import lax

BATCH = 1
CH = 10
GX = 256
GY = 256
GZ = 32
NT = 8
KX = 48
KY = 48
KZ = 24
KT = 4
KZT = 96
MODES = 4608
COEFS = 221184


def levels(stream_key, dims, split, low, top_value):
    def one(axis_at, shards_of):
        draws = jax.random.uniform(jax.random.fold_in(jax.random.fold_in(stream_key, 6), axis_at), (shards_of,), jnp.float32, low / len(split), top_value / len(split))
        return jnp.repeat(jnp.exp(draws), dims[axis_at] // shards_of).reshape((-1,) + (1,) * (len(dims) - axis_at - 1))

    gain = one(*split[0])
    for cut in split[1:]:
        gain = gain * one(*cut)
    return gain


def scatter_about(key, dims, width, most, pieces=(), kind=jnp.bfloat16):
    drawn = jax.random.normal(key, dims, jnp.float32) * width
    if len(pieces) > 0:
        drawn = levels(key, dims, pieces, -0.22, 0.18) * drawn
    return jnp.clip(drawn, min=-most, max=most).astype(kind)


def setup_inputs(seed: int = 0, part: int = 0) -> dict:
    streams_of = jax.random.split(jax.random.key(seed), 6)
    part_keys = jax.random.split(jax.random.fold_in(streams_of[5], part), 6)
    return {
        "features": scatter_about(part_keys[0], (BATCH, CH, GX, GY, GZ * NT), 1.0, 6.0, ((2, 32),)),
        "cotangent": scatter_about(part_keys[1], (BATCH, CH, GX, GY, GZ * NT), 1.0, 6.0, ((2, 32),)),
        "spectral_weight": scatter_about(streams_of[2], (2, CH, CH, COEFS), (2 * CH) ** -0.5, 1.25, ((3, 32),)),
        "pointwise_weight": scatter_about(streams_of[3], (CH, CH), CH ** -0.5, 2.0),
        "bias_term": scatter_about(streams_of[4], (CH,), 0.5, 3.0, (), jnp.float32),
    }


PRECISE = lax.Precision.HIGHEST

def depth_time_table():
    flat_ids = jnp.arange(GZ * NT, dtype=jnp.int32)
    depth_ids = flat_ids // NT
    time_ids = flat_ids % NT
    column_ids = jnp.arange(2 * KZT, dtype=jnp.int32)
    pair_ids = column_ids // 2
    depth_index = pair_ids // KT
    time_index = pair_ids % KT
    depth_freq = jnp.where(depth_index < KZ // 2, depth_index, GZ - KZ + depth_index)
    time_freq = jnp.where(time_index < KT // 2, time_index, NT - KT + time_index)
    phase_index = (depth_freq[None, :] * depth_ids[:, None] * NT + time_freq[None, :] * time_ids[:, None] * GZ) % (GZ * NT)
    angles = phase_index.astype(jnp.float32) * (2.0 * math.pi / (GZ * NT))
    return jnp.where((column_ids % 2)[None, :] == 0, jnp.cos(angles), -jnp.sin(angles)).astype(jnp.bfloat16)

def cross_tables():
    grid_ids = jnp.arange(GY, dtype=jnp.int32)
    freq_ids = jnp.arange(KY, dtype=jnp.int32)
    phase_index = grid_ids[:, None] * freq_ids[None, :] % GY
    angles = phase_index.astype(jnp.float32) * (2.0 * math.pi / GY)
    return (jnp.cos(angles).astype(jnp.bfloat16), jnp.sin(angles).astype(jnp.bfloat16))

def grid_tables():
    grid_ids = jnp.arange(GX, dtype=jnp.int32)
    freq_ids = jnp.arange(KX, dtype=jnp.int32)
    x_freq = jnp.where(freq_ids < KX // 2, freq_ids, GX - KX + freq_ids)
    phase_index = grid_ids[:, None] * x_freq[None, :] % GX
    angles = phase_index.astype(jnp.float32) * (2.0 * math.pi / GX)
    return (jnp.cos(angles).astype(jnp.bfloat16), jnp.sin(angles).astype(jnp.bfloat16))

def cross_doubling():
    freq_ids = jnp.arange(KY, dtype=jnp.int32)
    return jnp.where(freq_ids == 0, 1.0, 2.0).astype(jnp.bfloat16)

def mode_doubling():
    coef_ids = jnp.arange(COEFS, dtype=jnp.int32)
    return jnp.where(coef_ids // (KX * KZT) == 0, 1.0, 2.0).astype(jnp.float32)

def coef_rows(field, zt_basis, cos_y, sin_y):
    base = zt_basis.astype(jnp.float32)
    cross_cos = cos_y.astype(jnp.float32)
    cross_sin = sin_y.astype(jnp.float32)

    def one_plane(x_id):
        plane = lax.dynamic_index_in_dim(field, x_id, 2, keepdims=False).astype(jnp.float32)
        depth_coef = (jnp.einsum('bcyf,fn->bcyn', plane, base, precision=PRECISE) * (1.0 / math.sqrt(GZ * NT))).astype(jnp.bfloat16)
        depth_coef = lax.optimization_barrier(depth_coef).astype(jnp.float32)
        cos_part = jnp.einsum('bcyn,yk->bckn', depth_coef, cross_cos, precision=PRECISE).reshape(BATCH, CH, KY, KZT, 2)
        sin_part = jnp.einsum('bcyn,yk->bckn', depth_coef, cross_sin, precision=PRECISE).reshape(BATCH, CH, KY, KZT, 2)
        real_part = cos_part[..., 0] + sin_part[..., 1]
        imag_part = cos_part[..., 1] - sin_part[..., 0]
        joined = jnp.stack([real_part, imag_part], -1) * (1.0 / math.sqrt(GY))
        return joined.reshape(BATCH, CH, 2 * MODES).astype(jnp.bfloat16)
    planes = lax.map(one_plane, jnp.arange(GX, dtype=jnp.int32))
    return jnp.moveaxis(planes, 0, 2)

def to_modes(coefs, grid_cos, grid_sin):
    row_count = coefs.shape[0]
    split_parts = coefs.astype(jnp.float32).reshape(row_count, CH, GX, MODES, 2)
    cos_part = jnp.einsum('rcxmp,xk->rcmpk', split_parts, grid_cos.astype(jnp.float32), precision=PRECISE)
    sin_part = jnp.einsum('rcxmp,xk->rcmpk', split_parts, grid_sin.astype(jnp.float32), precision=PRECISE)
    grid_scale = 1.0 / math.sqrt(GX)
    real_part = (cos_part[:, :, :, 0] + sin_part[:, :, :, 1]) * grid_scale
    imag_part = (cos_part[:, :, :, 1] - sin_part[:, :, :, 0]) * grid_scale
    return (real_part.reshape(row_count, CH, COEFS), imag_part.reshape(row_count, CH, COEFS))

def spectral(feat_real, feat_imag, weight):
    weight_real = weight[0].astype(jnp.float32)
    weight_imag = weight[1].astype(jnp.float32)
    out_real = jnp.einsum('rcq,coq->roq', feat_real, weight_real, precision=PRECISE) - jnp.einsum('rcq,coq->roq', feat_imag, weight_imag, precision=PRECISE)
    out_imag = jnp.einsum('rcq,coq->roq', feat_real, weight_imag, precision=PRECISE) + jnp.einsum('rcq,coq->roq', feat_imag, weight_real, precision=PRECISE)
    return (out_real, out_imag)

def adjoint(cot_real, cot_imag, weight):
    weight_real = weight[0].astype(jnp.float32)
    weight_imag = weight[1].astype(jnp.float32)
    adj_real = jnp.einsum('roq,coq->rcq', cot_real, weight_real, precision=PRECISE) + jnp.einsum('roq,coq->rcq', cot_imag, weight_imag, precision=PRECISE)
    adj_imag = jnp.einsum('roq,coq->rcq', cot_imag, weight_real, precision=PRECISE) - jnp.einsum('roq,coq->rcq', cot_real, weight_imag, precision=PRECISE)
    return (adj_real, adj_imag)

def weight_grads(feat_real, feat_imag, cot_real, cot_imag, doubling):
    grad_real = (jnp.einsum('rcq,roq->coq', feat_real, cot_real, precision=PRECISE) + jnp.einsum('rcq,roq->coq', feat_imag, cot_imag, precision=PRECISE)) * doubling
    grad_imag = (jnp.einsum('rcq,roq->coq', feat_real, cot_imag, precision=PRECISE) - jnp.einsum('rcq,roq->coq', feat_imag, cot_real, precision=PRECISE)) * doubling
    return jnp.stack([grad_real, grad_imag], 0)

def to_grid(real_part, imag_part, grid_cos, grid_sin):
    row_count = real_part.shape[0]
    mode_count = real_part.shape[2] // KX
    stacked = jnp.stack([real_part, imag_part], 2).astype(jnp.bfloat16).reshape(row_count, CH, 2, mode_count, KX)
    stacked = lax.optimization_barrier(stacked).astype(jnp.float32)
    cos_part = jnp.einsum('rcpmk,xk->rcxmp', stacked, grid_cos.astype(jnp.float32), precision=PRECISE)
    sin_part = jnp.einsum('rcpmk,xk->rcxmp', stacked, grid_sin.astype(jnp.float32), precision=PRECISE)
    pen_real = cos_part[..., 0] - sin_part[..., 1]
    pen_imag = sin_part[..., 0] + cos_part[..., 1]
    joined = jnp.stack([pen_real, pen_imag], -1) * (1.0 / math.sqrt(GX))
    return joined.astype(jnp.bfloat16).reshape(row_count, CH, GX, 2 * mode_count)

def space_rows(pencil, field, zt_basis, cos_y, sin_y, pointwise_weight, shift, pattern):
    base = zt_basis.astype(jnp.float32)
    cross_cos = cos_y.astype(jnp.float32)
    cross_sin = sin_y.astype(jnp.float32)
    doubling_rows = cross_doubling().astype(jnp.float32)
    point = pointwise_weight.astype(jnp.float32)

    def one_plane(x_id):
        pencil_row = lax.dynamic_index_in_dim(pencil, x_id, 2, keepdims=False).astype(jnp.float32)
        weighted = pencil_row.reshape(BATCH, CH, KY, 2 * KZT) * doubling_rows[None, None, :, None]
        cos_part = jnp.einsum('bckn,yk->bcyn', weighted, cross_cos, precision=PRECISE).reshape(BATCH, CH, GY, KZT, 2)
        sin_part = jnp.einsum('bckn,yk->bcyn', weighted, cross_sin, precision=PRECISE).reshape(BATCH, CH, GY, KZT, 2)
        u_real = cos_part[..., 0] - sin_part[..., 1]
        u_imag = sin_part[..., 0] + cos_part[..., 1]
        joined = (jnp.stack([u_real, u_imag], -1) * (1.0 / math.sqrt(GY))).reshape(BATCH, CH, GY, 2 * KZT).astype(jnp.bfloat16)
        joined = lax.optimization_barrier(joined).astype(jnp.float32)
        spatial = jnp.einsum('bcyn,fn->bcyf', joined, base, precision=PRECISE) * (1.0 / math.sqrt(GZ * NT))
        data_plane = lax.dynamic_index_in_dim(field, x_id, 2, keepdims=False).astype(jnp.float32)
        local_mix = jnp.einsum(pattern, data_plane, point, precision=PRECISE)
        return (spatial + local_mix + shift[None, :, None, None]).astype(jnp.bfloat16)
    planes = lax.map(one_plane, jnp.arange(GX, dtype=jnp.int32))
    return jnp.moveaxis(planes, 0, 2)

def reference(features, cotangent, spectral_weight, pointwise_weight, bias_term):
    zt_basis = depth_time_table()
    cos_y, sin_y = cross_tables()
    grid_cos, grid_sin = grid_tables()
    doubling = mode_doubling()
    feat_real, feat_imag = to_modes(coef_rows(features, zt_basis, cos_y, sin_y), grid_cos, grid_sin)
    cot_real, cot_imag = to_modes(coef_rows(cotangent, zt_basis, cos_y, sin_y), grid_cos, grid_sin)
    out_real, out_imag = spectral(feat_real, feat_imag, spectral_weight)
    adj_real, adj_imag = adjoint(cot_real, cot_imag, spectral_weight)
    weight_grad = weight_grads(feat_real, feat_imag, cot_real, cot_imag, doubling)
    pen_y = to_grid(out_real, out_imag, grid_cos, grid_sin)
    pen_d = to_grid(adj_real, adj_imag, grid_cos, grid_sin)
    layer_out = space_rows(pen_y, features, zt_basis, cos_y, sin_y, pointwise_weight, bias_term, 'bcyf,co->boyf')
    zero_shift = jnp.zeros((CH,), jnp.float32)
    feature_grad = space_rows(pen_d, cotangent, zt_basis, cos_y, sin_y, pointwise_weight, zero_shift, 'boyf,co->bcyf')
    return (layer_out, feature_grad, weight_grad)
```

```python
import math

import jax
import jax.numpy as jnp
from jax import lax
from jax.experimental import pallas as pl
from jax.experimental.pallas import tpu as pltpu
from jax.sharding import PartitionSpec as P

GX = 256
GY = 256
GZ = 32
NT = 8
KX = 48
KY = 48
KZ = 24
KT = 4
KZT = 96
MODES = 4608


PRECISE = lax.Precision.HIGHEST


def depth_time_table():
    flat_ids = jnp.arange(GZ * NT, dtype=jnp.int32)
    depth_ids = flat_ids // NT
    time_ids = flat_ids % NT
    column_ids = jnp.arange(2 * KZT, dtype=jnp.int32)
    part_ids = column_ids // KZT
    pair_ids = column_ids % KZT
    depth_index = pair_ids // KT
    time_index = pair_ids % KT
    depth_freq = jnp.where(depth_index < KZ // 2, depth_index, GZ - KZ + depth_index)
    time_freq = jnp.where(time_index < KT // 2, time_index, NT - KT + time_index)
    phase_index = (
        depth_freq[None, :] * depth_ids[:, None] * NT + time_freq[None, :] * time_ids[:, None] * GZ
    ) % (GZ * NT)
    angles = phase_index.astype(jnp.float32) * (2.0 * math.pi / (GZ * NT))
    return jnp.where(part_ids[None, :] == 0, jnp.cos(angles), -jnp.sin(angles)).astype(jnp.bfloat16)


def cross_tables():
    grid_ids = jnp.arange(GY, dtype=jnp.int32)
    freq_ids = jnp.arange(KY, dtype=jnp.int32)
    phase_index = grid_ids[:, None] * freq_ids[None, :] % GY
    angles = phase_index.astype(jnp.float32) * (2.0 * math.pi / GY)
    return (jnp.cos(angles).astype(jnp.bfloat16), jnp.sin(angles).astype(jnp.bfloat16))


def grid_tables():
    grid_ids = jnp.arange(GX, dtype=jnp.int32)
    freq_ids = jnp.arange(KX, dtype=jnp.int32)
    x_freq = jnp.where(freq_ids < KX // 2, freq_ids, GX - KX + freq_ids)
    phase_index = grid_ids[:, None] * x_freq[None, :] % GX
    angles = phase_index.astype(jnp.float32) * (2.0 * math.pi / GX)
    return (jnp.cos(angles).astype(jnp.bfloat16), jnp.sin(angles).astype(jnp.bfloat16))


def cross_doubling():
    freq_ids = jnp.arange(KY, dtype=jnp.int32)
    return jnp.where(freq_ids == 0, 1.0, 2.0).astype(jnp.bfloat16)


def to_coefs(field, depth_order, cross_pair):
    row_count, channels, xlocal = (field.shape[0], field.shape[1], field.shape[2])
    depth_coef = jnp.einsum(
        "rcxyf,fn->rcxyn", field, depth_order, preferred_element_type=jnp.float32
    )
    depth_coef = (depth_coef * (1.0 / math.sqrt(GZ * NT))).astype(jnp.bfloat16)
    products = jnp.einsum(
        "rcxyn,yk->rcxkn", depth_coef, cross_pair, preferred_element_type=jnp.float32
    )
    real_part = products[:, :, :, :KY, :KZT] + products[:, :, :, KY:, KZT:]
    imag_part = products[:, :, :, :KY, KZT:] - products[:, :, :, KY:, :KZT]
    joined = jnp.stack([real_part, imag_part], 3) * (1.0 / math.sqrt(GY))
    return joined.reshape(row_count, channels, xlocal, 2, MODES).astype(jnp.bfloat16)


def gather_modes(coefs, grid_pair):
    row_count, channels, xlocal = (coefs.shape[0], coefs.shape[1], coefs.shape[2])
    mode_local = MODES // lax.axis_size("px")
    grid_scale = 1.0 / math.sqrt(GX)
    received = lax.all_to_all(coefs, "px", split_axis=4, concat_axis=2, tiled=True)
    products = jnp.einsum(
        "rcxpm,xk->rcpmk", received, grid_pair, preferred_element_type=jnp.float32
    )
    real_part = (products[:, :, 0, :, :KX] + products[:, :, 1, :, KX:]) * grid_scale
    imag_part = (products[:, :, 1, :, :KX] - products[:, :, 0, :, KX:]) * grid_scale
    return (
        real_part.reshape(row_count, channels, mode_local * KX),
        imag_part.reshape(row_count, channels, mode_local * KX),
    )


def spectral(feat_real, feat_imag, weight):
    weight_real = weight[0].astype(jnp.float32)
    weight_imag = weight[1].astype(jnp.float32)
    out_real = jnp.einsum("rcq,coq->roq", feat_real, weight_real, precision=PRECISE) - jnp.einsum(
        "rcq,coq->roq", feat_imag, weight_imag, precision=PRECISE
    )
    out_imag = jnp.einsum("rcq,coq->roq", feat_real, weight_imag, precision=PRECISE) + jnp.einsum(
        "rcq,coq->roq", feat_imag, weight_real, precision=PRECISE
    )
    return (out_real, out_imag)


def adjoint(cot_real, cot_imag, weight):
    weight_real = weight[0].astype(jnp.float32)
    weight_imag = weight[1].astype(jnp.float32)
    adj_real = jnp.einsum("roq,coq->rcq", cot_real, weight_real, precision=PRECISE) + jnp.einsum(
        "roq,coq->rcq", cot_imag, weight_imag, precision=PRECISE
    )
    adj_imag = jnp.einsum("roq,coq->rcq", cot_imag, weight_real, precision=PRECISE) - jnp.einsum(
        "roq,coq->rcq", cot_real, weight_imag, precision=PRECISE
    )
    return (adj_real, adj_imag)


def weight_grads(feat_real, feat_imag, cot_real, cot_imag, doubling, stack_axis=0):
    grad_real = (
        jnp.einsum("rcq,roq->coq", feat_real, cot_real, precision=PRECISE)
        + jnp.einsum("rcq,roq->coq", feat_imag, cot_imag, precision=PRECISE)
    ) * doubling
    grad_imag = (
        jnp.einsum("rcq,roq->coq", feat_real, cot_imag, precision=PRECISE)
        - jnp.einsum("rcq,roq->coq", feat_imag, cot_real, precision=PRECISE)
    ) * doubling
    return jnp.stack([grad_real, grad_imag], stack_axis)


def grid_back(real_part, imag_part, grid_cos, grid_sin, depth_order, cos_y, sin_y, doubling_rows):
    row_count, channels, coef_local = real_part.shape
    mode_local = coef_local // KX
    stacked = (
        jnp.stack([real_part, imag_part], 2)
        .astype(jnp.bfloat16)
        .reshape(row_count, channels, 2, mode_local, KX)
    )
    cos_part = jnp.einsum("rcpmk,xk->rcxpm", stacked, grid_cos, preferred_element_type=jnp.float32)
    sin_part = jnp.einsum("rcpmk,xk->rcxpm", stacked, grid_sin, preferred_element_type=jnp.float32)
    pen_real = cos_part[:, :, :, 0] - sin_part[:, :, :, 1]
    pen_imag = sin_part[:, :, :, 0] + cos_part[:, :, :, 1]
    pencil = (jnp.stack([pen_real, pen_imag], 3) * (1.0 / math.sqrt(GX))).astype(jnp.bfloat16)
    returned = lax.all_to_all(pencil, "px", split_axis=2, concat_axis=4, tiled=True)
    xlocal = returned.shape[2]
    weighted = (
        returned.reshape(row_count, channels, xlocal, 2, KY, KZT)
        * doubling_rows[None, None, None, None, :, None]
    )
    cross_cos = jnp.einsum("rcxpkw,yk->rcxypw", weighted, cos_y, preferred_element_type=jnp.float32)
    cross_sin = jnp.einsum("rcxpkw,yk->rcxypw", weighted, sin_y, preferred_element_type=jnp.float32)
    u_real = cross_cos[:, :, :, :, 0] - cross_sin[:, :, :, :, 1]
    u_imag = cross_sin[:, :, :, :, 0] + cross_cos[:, :, :, :, 1]
    spread = (jnp.concatenate([u_real, u_imag], -1) * (1.0 / math.sqrt(GY))).astype(jnp.bfloat16)
    summed = jnp.einsum("rcxyn,fn->rcxyf", spread, depth_order, preferred_element_type=jnp.float32)
    return summed * (1.0 / math.sqrt(GZ * NT))


def shards(features, cotangent, spectral_weight, pointwise_weight, bias_term):
    depth_order = depth_time_table()
    cos_y, sin_y = cross_tables()
    cross_pair = jnp.concatenate([cos_y, sin_y], 1)
    grid_cos, grid_sin = grid_tables()
    grid_pair = jnp.concatenate([grid_cos, grid_sin], 1)
    doubling_rows = cross_doubling()
    coef_local = spectral_weight.shape[3]
    mode_local = coef_local // KX
    local_mode = lax.axis_index("px") * mode_local + jnp.arange(coef_local, dtype=jnp.int32) // KX
    doubling = jnp.where(local_mode // KZT == 0, 1.0, 2.0).astype(jnp.float32)
    coef_in = to_coefs(features, depth_order, cross_pair)
    coef_cot = to_coefs(cotangent, depth_order, cross_pair)
    feat_real, feat_imag = gather_modes(coef_in, grid_pair)
    out_real, out_imag = spectral(feat_real, feat_imag, spectral_weight)
    back_y = grid_back(
        out_real, out_imag, grid_cos, grid_sin, depth_order, cos_y, sin_y, doubling_rows
    )
    cot_real, cot_imag = gather_modes(coef_cot, grid_pair)
    adj_real, adj_imag = adjoint(cot_real, cot_imag, spectral_weight)
    back_d = grid_back(
        adj_real, adj_imag, grid_cos, grid_sin, depth_order, cos_y, sin_y, doubling_rows
    )
    weight_grad = weight_grads(feat_real, feat_imag, cot_real, cot_imag, doubling)
    layer_out = (
        back_y
        + jnp.einsum(
            "rcxyf,co->roxyf", features, pointwise_weight, preferred_element_type=jnp.float32
        )
        + bias_term[None, :, None, None, None]
    )
    input_grad = back_d + jnp.einsum(
        "roxyf,co->rcxyf", cotangent, pointwise_weight, preferred_element_type=jnp.float32
    )
    return (layer_out.astype(jnp.bfloat16), input_grad.astype(jnp.bfloat16), weight_grad)


LANE = 128
ROWS = 16


def interleaved_rows(table):
    return table.reshape(table.shape[0], KY // 3, 3).transpose(0, 2, 1).reshape(table.shape[0], KY)


def padded_depth(depth_order):
    gap = ((0, 0), (0, LANE - KZT))
    return jnp.concatenate(
        [jnp.pad(depth_order[:, :KZT], gap), jnp.pad(depth_order[:, KZT:], gap)], 1
    )


def coef_body(field_ref, depth_ref, cross_ref, out_ref, even_ref, odd_ref):
    xlocal = field_ref.shape[2]
    third = KY // 3
    half = KZT // 2
    block = KZT + half
    for x in range(xlocal):
        depth_coef = jnp.dot(
            field_ref[0, 0, x], depth_ref[...], preferred_element_type=jnp.float32
        )
        depth_coef = (depth_coef * (1.0 / math.sqrt(GZ * NT))).astype(jnp.bfloat16)
        products = jnp.dot(cross_ref[...], depth_coef, preferred_element_type=jnp.float32)
        parts = (
            products[:KY, :LANE] + products[KY:, LANE:],
            products[:KY, LANE:] - products[KY:, :LANE],
        )
        for p, part in enumerate(parts):
            part = part * (1.0 / math.sqrt(GY))
            first, second, last = (part[r * third : (r + 1) * third, :KZT] for r in range(3))
            even = jnp.concatenate([first, second[:, :half]], 1)
            odd = jnp.concatenate([second[:, half:], last], 1)
            even_ref[x, :, p * block : (p + 1) * block] = even
            odd_ref[x, :, p * block : (p + 1) * block] = odd
    for c in range(out_ref.shape[2] // (2 * block)):

        @pl.when(pl.program_id(0) == c)
        def _():
            for j in range(third):
                lanes = slice(c * 2 * block, (c + 1) * 2 * block)
                out_ref[2 * j, :, lanes] = even_ref[:, j, :].astype(jnp.bfloat16)
                out_ref[2 * j + 1, :, lanes] = odd_ref[:, j, :].astype(jnp.bfloat16)


def coef_kernel(field, depth_pad, cross_rows):
    _, channels, xlocal, gy, zt = field.shape
    block = KZT + KZT // 2
    blocks = MODES // block
    return pl.pallas_call(
        coef_body,
        grid=(channels,),
        in_specs=[
            pl.BlockSpec((1, 1, xlocal, gy, zt), lambda c: (0, c, 0, 0, 0)),
            pl.BlockSpec(depth_pad.shape, lambda c: (0, 0)),
            pl.BlockSpec(cross_rows.shape, lambda c: (0, 0)),
        ],
        out_specs=pl.BlockSpec((blocks, xlocal, channels * 2 * block), lambda c: (0, 0, 0)),
        out_shape=jax.ShapeDtypeStruct((blocks, xlocal, channels * 2 * block), jnp.bfloat16),
        scratch_shapes=[
            pltpu.VMEM((xlocal, KY // 3, 2 * block), jnp.float32),
            pltpu.VMEM((xlocal, KY // 3, 2 * block), jnp.float32),
        ],
        compiler_params=pltpu.CompilerParams(vmem_limit_bytes=56 * 2**20),
        cost_estimate=pl.CostEstimate(
            flops=30_000_000 * channels * xlocal, bytes_accessed=14_000_000, transcendentals=0
        ),
    )(field, depth_pad, cross_rows)


def space_body(pencil_ref, field_ref, pair_ref, depth_ref, mix_ref, shift_ref, out_ref, back_ref):
    channels = field_ref.shape[1]
    half = KZT // 2
    block = KZT + half
    gap = jnp.zeros((KY, LANE - KZT), jnp.bfloat16)

    def spread_rows(p, c):
        offset = (p * channels + c) * block
        even = pencil_ref[0, 0, :, offset : offset + block]
        odd = pencil_ref[0, 1, :, offset : offset + block]
        second = jnp.concatenate([even[:, KZT:], odd[:, :half]], 1)
        rows = jnp.concatenate([even[:, :KZT], second, odd[:, half:]], 0)
        return jnp.concatenate([rows, gap], 1)

    for c in range(channels):
        real_rows = spread_rows(0, c)
        imag_rows = spread_rows(1, c)
        both = jnp.concatenate(
            [
                jnp.concatenate([real_rows, imag_rows], 1),
                jnp.concatenate([-imag_rows, real_rows], 1),
            ],
            0,
        )
        spread = jnp.dot(pair_ref[...], both, preferred_element_type=jnp.float32)
        spread = (spread * (1.0 / math.sqrt(GY))).astype(jnp.bfloat16)
        back_ref[c] = jnp.dot(spread, depth_ref[...], preferred_element_type=jnp.float32) * (
            1.0 / math.sqrt(GZ * NT)
        )
    gy, zt = field_ref.shape[3], field_ref.shape[4]
    for y in range(0, gy, ROWS):
        rows = slice(y, y + ROWS)
        tile = field_ref[0, :, 0, rows, :].reshape(channels * ROWS, zt)
        mixed = jnp.dot(mix_ref[...], tile, preferred_element_type=jnp.float32)
        mixed = (mixed + shift_ref[...]).reshape(channels, ROWS, zt)
        out_ref[0, :, 0, rows, :] = (back_ref[:, rows, :] + mixed).astype(jnp.bfloat16)


def space_kernel(pencil, field, pair_rows, depth_rows, mix, shift):
    _, channels, xlocal, gy, zt = field.shape
    plane = pl.BlockSpec((1, channels, 1, gy, zt), lambda x: (0, 0, x, 0, 0))
    return pl.pallas_call(
        space_body,
        grid=(xlocal,),
        in_specs=[
            pl.BlockSpec((1,) + pencil.shape[1:], lambda x: (x, 0, 0, 0)),
            plane,
            pl.BlockSpec(pair_rows.shape, lambda x: (0, 0)),
            pl.BlockSpec(depth_rows.shape, lambda x: (0, 0)),
            pl.BlockSpec(mix.shape, lambda x: (0, 0)),
            pl.BlockSpec(shift.shape, lambda x: (0, 0)),
        ],
        out_specs=plane,
        out_shape=jax.ShapeDtypeStruct(field.shape, jnp.bfloat16),
        scratch_shapes=[pltpu.VMEM((channels, gy, zt), jnp.float32)],
        compiler_params=pltpu.CompilerParams(vmem_limit_bytes=56 * 2**20),
        cost_estimate=pl.CostEstimate(
            flops=60_000_000 * channels * xlocal, bytes_accessed=24_000_000, transcendentals=0
        ),
    )(pencil, field, pair_rows, depth_rows, mix, shift)


def modes_of(received, grid_pair, channels, mode_local):
    products = jnp.einsum("xn,xk->nk", received, grid_pair, preferred_element_type=jnp.float32)
    products = products.reshape(channels, 2, mode_local, 2 * KX)
    grid_scale = 1.0 / math.sqrt(GX)
    real_part = (products[:, 0, :, :KX] + products[:, 1, :, KX:]) * grid_scale
    imag_part = (products[:, 1, :, :KX] - products[:, 0, :, KX:]) * grid_scale
    return (
        real_part.reshape(1, channels, mode_local * KX),
        imag_part.reshape(1, channels, mode_local * KX),
    )


def pencils_of(real_part, imag_part, grid_cos, grid_sin, mode_local):
    channels = real_part.shape[1]
    real_rows = real_part.astype(jnp.bfloat16).reshape(channels * mode_local, KX)
    imag_rows = imag_part.astype(jnp.bfloat16).reshape(channels * mode_local, KX)
    joined = jnp.concatenate([real_rows, imag_rows], 1)
    pen_real = jnp.einsum(
        "xk,nk->xn",
        jnp.concatenate([grid_cos, -grid_sin], 1),
        joined,
        preferred_element_type=jnp.float32,
    )
    pen_imag = jnp.einsum(
        "xk,nk->xn",
        jnp.concatenate([grid_sin, grid_cos], 1),
        joined,
        preferred_element_type=jnp.float32,
    )
    pencil = jnp.concatenate([pen_real, pen_imag], 1) * (1.0 / math.sqrt(GX))
    return pencil.astype(jnp.bfloat16)


def block_shards(features, cotangent, spectral_weight, pointwise_weight, bias_term):
    channels, xlocal = features.shape[1], features.shape[2]
    mode_local = spectral_weight.shape[3] // KX
    blocks = MODES // mode_local
    depth_order = depth_time_table()
    depth_pad = padded_depth(depth_order)
    cos_y, sin_y = (interleaved_rows(table) for table in cross_tables())
    cross_rows = jnp.concatenate([cos_y, sin_y], 1).T
    twice = interleaved_rows(cross_doubling()[None, :])
    pair_rows = jnp.concatenate([cos_y * twice, sin_y * twice], 1)
    grid_cos, grid_sin = grid_tables()
    grid_pair = jnp.concatenate([grid_cos, grid_sin], 1)
    local_mode = lax.axis_index("px") * mode_local + jnp.arange(
        mode_local * KX, dtype=jnp.int32
    ) // KX
    doubling = jnp.where(local_mode // KZT == 0, 1.0, 2.0).astype(jnp.float32)

    def forth(field):
        coefs = coef_kernel(field, depth_pad, cross_rows)
        received = lax.all_to_all(coefs, "px", split_axis=0, concat_axis=0, tiled=True)
        return received.reshape(blocks * xlocal, coefs.shape[2])

    def exchange(pencil):
        sent = pencil.reshape(blocks, xlocal, pencil.shape[1])
        return lax.all_to_all(sent, "px", split_axis=0, concat_axis=0, tiled=True)

    def back(returned, field, mix, shift):
        returned = returned.reshape(blocks // 2, 2, xlocal, returned.shape[2])
        returned = returned.transpose(2, 1, 0, 3)
        mix_rows = jnp.kron(mix, jnp.eye(ROWS, dtype=mix.dtype))
        shift_rows = jnp.broadcast_to(
            jnp.repeat(shift, ROWS)[:, None], (channels * ROWS, field.shape[4])
        )
        return space_kernel(returned, field, pair_rows, depth_pad.T, mix_rows, shift_rows)

    feat_coefs = forth(features)
    cot_coefs = forth(cotangent)
    feat_real, feat_imag = modes_of(feat_coefs, grid_pair, channels, mode_local)
    out_real, out_imag = spectral(feat_real, feat_imag, spectral_weight)
    pen_y = pencils_of(out_real, out_imag, grid_cos, grid_sin, mode_local)
    cot_coefs, pen_y = lax.optimization_barrier((cot_coefs, pen_y))
    returned_y = exchange(pen_y)
    cot_real, cot_imag = modes_of(cot_coefs, grid_pair, channels, mode_local)
    adj_real, adj_imag = adjoint(cot_real, cot_imag, spectral_weight)
    pen_d = pencils_of(adj_real, adj_imag, grid_cos, grid_sin, mode_local)
    weight_grad = weight_grads(feat_real, feat_imag, cot_real, cot_imag, doubling, 2)
    pen_d, weight_grad = lax.optimization_barrier((pen_d, weight_grad))
    returned_d = exchange(pen_d)
    layer_out = back(returned_y, features, pointwise_weight.T, bias_term)
    returned_d, layer_out = lax.optimization_barrier((returned_d, layer_out))
    input_grad = back(returned_d, cotangent, pointwise_weight, jnp.zeros_like(bias_term))
    return (layer_out, input_grad, weight_grad.transpose(2, 0, 1, 3))


def any_shards(features, cotangent, spectral_weight, pointwise_weight, bias_term):
    whole_tiles = features.shape[0] == 1 and features.shape[2] % 8 == 0
    if whole_tiles and 2 * spectral_weight.shape[3] == 3 * KZT * KX:
        return block_shards(features, cotangent, spectral_weight, pointwise_weight, bias_term)
    return shards(features, cotangent, spectral_weight, pointwise_weight, bias_term)


def solution(mesh):
    in_specs = (
        P("groups", None, "px", None, None),
        P("groups", None, "px", None, None),
        P(None, None, None, "px"),
        P(),
        P(),
    )
    out_specs = (
        P("groups", None, "px", None, None),
        P("groups", None, "px", None, None),
        P("groups", None, None, "px"),
    )
    return jax.shard_map(any_shards, mesh=mesh, in_specs=in_specs, out_specs=out_specs, check_vma=False)
```
